32 devices in a mesh: exp: 4 (over y, core), seq: 2 (over x), dp: 4 (over z).
Axes of the slice: x: 2, y: 2, z: 4, core: 2. Of those that a mesh axis runs over, the one named last changes fastest.
Arguments:
- queries: bfloat16 [4, 256, 4, 2048], P('exp', None, 'dp', 'seq'), may hold values from -160 to 160
- latent_rows: bfloat16 [4, 256, 512], P('exp'), may hold values from -8 to 8
- key_weight: bfloat16 [512, 4, 2048], P(None, 'dp', 'seq'), may hold values from -1 to 1
- output_grad: bfloat16 [4, 256, 4, 2048], P('exp', 'seq', 'dp'), may hold values from -6 to 6
- down_weight: bfloat16 [4, 2048, 7168], P('exp', 'dp', 'seq'), may hold values from -0.125 to 0.125
- hidden_rows: bfloat16 [768, 2048], P('exp', 'dp'), may hold values from -6 to 6
- upstream_rows: bfloat16 [768, 7168], P('exp', 'seq'), may hold values from -6 to 6
- row_gates: float32 [768], P('exp'), may hold values from 0.03 to 0.5
- row_counts: int32 [4, 3], P('exp'), may hold values from 0 to 64, as said below
Outputs:
- value_grad: bfloat16 [4, 256, 4, 2048], P('exp', None, 'dp', 'seq')
- hidden_grad: float32 [768, 2048], P(('exp', 'seq'), 'dp')
- weight_grad: bfloat16 [4, 2048, 7168], P('exp', 'dp', 'seq')
The draws below stay inside these ranges and needn't reach their ends.
Inputs may be any that keep to these rules, and one draw needn't show every extreme that they name: `row_counts`: A block with 0 live rows means host j keeps no copy of expert e(j, b); in every draw some block is full with 64 live rows.
All inputs are finite; a program needn't handle non-finite values.
Results may differ from the reference program's by a relative error of at most 0.012.
The reference program's roundings to bfloat16 on the way count: a program that leaves them out, or rounds other values in their place, can miss the bound.
Values may be sent and summed in bfloat16 or wider, within the bound.
A program may use at most 64 MiB of HBM per device.

```python
import math
import jax
import jax.numpy as jnp
from jax import lax

D = 7168
FF = 2048
HEADS = 64
HEAD_DIM = 128
LATENT = 512
CAP = 64
EXPERTS = 4
SEQS = 4
S_LEN = 256
STRIDE = 1
ROWS = 768
N_DP = 4


def attention_draws(key):
    latent_key = jax.random.fold_in(key, 101)
    weight_key = jax.random.fold_in(key, 102)
    query_key = jax.random.fold_in(key, 103)
    group_width = HEADS // N_DP * HEAD_DIM
    latent_draw = jnp.clip(jax.random.normal(latent_key, (SEQS, S_LEN, LATENT), jnp.float32), -6.0, 6.0)
    projection = jnp.clip(jax.random.normal(weight_key, (LATENT, N_DP, group_width), jnp.float32), -6.0, 6.0) / math.sqrt(LATENT)
    query_draw = jnp.clip(jax.random.normal(query_key, (SEQS, S_LEN, N_DP, group_width), jnp.float32), -6.0, 6.0)
    return (latent_draw, projection, query_draw)


def draw_queries(key, part):
    return attention_draws(key)[2].astype(jnp.bfloat16)


def draw_latent_rows(key, part):
    return attention_draws(key)[0].astype(jnp.bfloat16)


def draw_key_weight(key, part):
    return attention_draws(key)[1].astype(jnp.bfloat16)


def draw_row_counts(key, part):
    base_key = jax.random.fold_in(key, 201)
    full_key = jax.random.fold_in(key, 202)
    empty_key = jax.random.fold_in(key, 203)
    host_key = jax.random.fold_in(key, 204)
    base_counts = jax.random.randint(base_key, (EXPERTS, 3), CAP // 4, CAP // 2 + 1)
    full_block = jax.random.randint(full_key, (EXPERTS, 3), 0, 8) == 0
    empty_block = (jax.random.randint(empty_key, (EXPERTS, 3), 0, 4) == 0) & (jnp.arange(3)[None, :] > 0)
    counts_drawn = jnp.where(full_block, CAP, base_counts)
    counts_drawn = jnp.where(empty_block, 0, counts_drawn)
    chosen_host = jax.random.randint(host_key, (), 0, EXPERTS)
    return counts_drawn.at[chosen_host, 0].set(CAP).astype(jnp.int32)


def block_levels(rng, shape, cuts, low, top_value):
    factor_of, own = 1.0, jax.random.fold_in(rng, 6)
    for dim, blocks in cuts:
        draws = jnp.exp(jax.random.uniform(jax.random.fold_in(own, dim), (blocks,), jnp.float32, low / len(cuts), top_value / len(cuts)))
        factor_of = factor_of * jnp.repeat(draws, shape[dim] // blocks).reshape([-1 if axis == dim else 1 for axis in range(len(shape))])
    return factor_of


def centred(rng, dims, spread, limit, cuts=(), kind=jnp.bfloat16):
    drawn = spread * jax.random.normal(rng, dims, jnp.float32)
    if cuts:
        drawn = drawn * block_levels(rng, dims, cuts, -0.22, 0.18)
    return jnp.clip(drawn, -limit, limit).astype(kind)


def setup_inputs(seed: int = 0) -> dict:
    splits = jax.random.split(jax.random.key(seed), 10)
    queries = draw_queries(jax.random.fold_in(splits[9], 71), 0)
    latent_rows = draw_latent_rows(jax.random.fold_in(splits[9], 71), 0)
    key_weight = draw_key_weight(jax.random.fold_in(splits[9], 71), 0)
    output_grad = centred(splits[3], (SEQS, S_LEN, N_DP, HEADS // N_DP * HEAD_DIM), 1.0, 6.0, ((0, 4), (1, 2), (2, 4)))
    down_weight = centred(splits[4], (EXPERTS, FF, D), FF ** -0.5, 0.125, ((0, 4), (1, 4), (2, 2)))
    hidden_rows = centred(splits[5], (ROWS, FF), 1.0, 6.0, ((0, 4), (1, 4)))
    upstream_rows = centred(splits[6], (ROWS, D), 1.0, 6.0, ((0, 4), (1, 2)))
    row_gates = jnp.clip(jnp.exp(math.log(0.5) - 2.8134107 * jax.random.uniform(splits[7], (ROWS,), jnp.float32) ** block_levels(splits[7], (ROWS,), ((0, 4),), -0.2, 0.2)), 0.03, 0.5)
    row_counts = draw_row_counts(jax.random.fold_in(splits[9], 71), 0)
    return dict(queries=queries, latent_rows=latent_rows, key_weight=key_weight, output_grad=output_grad, down_weight=down_weight, hidden_rows=hidden_rows, upstream_rows=upstream_rows, row_gates=row_gates, row_counts=row_counts)


def one_head(inputs):
    query_head, key_head, grad_head = inputs
    score_scale = 1.0 / math.sqrt(HEAD_DIM)
    scores = jnp.dot(query_head, key_head.T, preferred_element_type=jnp.float32) * score_scale
    positions = jnp.arange(S_LEN)
    allowed = positions[None, :] <= positions[:, None]
    scores = jnp.where(allowed, scores, -jnp.inf)
    row_max = lax.optimization_barrier(jnp.max(scores, axis=1, keepdims=True))
    weights = jnp.exp(scores - row_max)
    softmax_rows = (weights / lax.optimization_barrier(jnp.sum(weights, axis=1, keepdims=True))).astype(jnp.bfloat16)
    return jnp.dot(softmax_rows.T, grad_head, preferred_element_type=jnp.float32).astype(jnp.bfloat16)

def attention_reference(queries, latent_rows, key_weight, output_grad):
    key_matrix = key_weight.reshape(LATENT, HEADS * HEAD_DIM)

    def one_sequence(inputs):
        latent_seq, query_seq, grad_seq = inputs
        key_rows = jnp.dot(latent_seq, key_matrix, preferred_element_type=jnp.float32).astype(jnp.bfloat16)
        key_heads = key_rows.reshape(S_LEN, HEADS, HEAD_DIM).transpose(1, 0, 2)
        query_heads = query_seq.reshape(S_LEN, HEADS, HEAD_DIM).transpose(1, 0, 2)
        grad_heads = grad_seq.reshape(S_LEN, HEADS, HEAD_DIM).transpose(1, 0, 2)
        result = lax.map(one_head, (query_heads, key_heads, grad_heads))
        return result.transpose(1, 0, 2).reshape(S_LEN, HEADS * HEAD_DIM)
    value_grad = lax.map(one_sequence, (latent_rows, queries.reshape(SEQS, S_LEN, HEADS * HEAD_DIM), output_grad.reshape(SEQS, S_LEN, HEADS * HEAD_DIM)))
    return value_grad.reshape(SEQS, S_LEN, N_DP, HEADS // N_DP * HEAD_DIM)

def expert_reference(down_weight, hidden_rows, upstream_rows, row_gates, row_counts):
    host_ids = jnp.arange(EXPERTS, dtype=jnp.int32)
    live_rows = jnp.arange(CAP, dtype=jnp.int32)[None, None, :] < row_counts[:, :, None]
    row_scale = jnp.where(live_rows, row_gates.reshape(EXPERTS, 3, CAP), jnp.zeros((), row_gates.dtype))
    hidden_blocks = hidden_rows.reshape(EXPERTS, 3, CAP, FF)
    upstream_blocks = upstream_rows.reshape(EXPERTS, 3, CAP, D)
    scaled_rows = (row_scale[..., None] * hidden_blocks.astype(jnp.float32)).astype(jnp.bfloat16)

    def host_grad(inputs):
        host_index, upstream_host, scale_host = inputs
        pieces = []
        for block_index in range(3):
            expert = (host_index - block_index * STRIDE) % EXPERTS
            matrix = lax.dynamic_index_in_dim(down_weight, expert, 0, keepdims=False)
            product = jnp.dot(upstream_host[block_index], matrix.T, preferred_element_type=jnp.float32)
            pieces.append(product * scale_host[block_index][:, None])
        return jnp.concatenate(pieces, 0)
    hidden_grad = lax.map(host_grad, (host_ids, upstream_blocks, row_scale)).reshape(ROWS, FF)

    def expert_grad(expert):
        summed = jnp.zeros((FF, D), jnp.float32)
        for block_index in range(3):
            host_index = (expert + block_index * STRIDE) % EXPERTS
            chosen_rows = lax.dynamic_index_in_dim(scaled_rows, host_index, 0, keepdims=False)[block_index]
            upstream = lax.dynamic_index_in_dim(upstream_blocks, host_index, 0, keepdims=False)[block_index]
            block_term = jnp.dot(chosen_rows.T, upstream, preferred_element_type=jnp.float32).astype(jnp.bfloat16)
            summed = summed + lax.optimization_barrier(block_term).astype(jnp.float32)
        return summed.astype(jnp.bfloat16)
    weight_grad = lax.map(expert_grad, host_ids)
    return (hidden_grad, weight_grad)

def reference(queries, latent_rows, key_weight, output_grad, down_weight, hidden_rows, upstream_rows, row_gates, row_counts):
    value_grad = attention_reference(queries, latent_rows, key_weight, output_grad)
    hidden_grad, weight_grad = expert_reference(down_weight, hidden_rows, upstream_rows, row_gates, row_counts)
    return (value_grad, hidden_grad, weight_grad)
```

```python
import functools
import math

import jax
import jax.numpy as jnp
from jax import lax
from jax.experimental import pallas as pl
from jax.experimental.pallas import tpu as pltpu
from jax.sharding import PartitionSpec as P

HEAD_DIM = 128
BLOCKS = 3
MESH = pl.DeviceIdType.MESH
LAST = (((1,), (1,)), ((), ()))


def dot_of(a, b):
    return jnp.dot(a, b, preferred_element_type=jnp.float32)


def grad_groups(capacity, rows_per):
    granule = math.gcd(capacity, rows_per)
    groups = []
    for block in range(BLOCKS):
        row, end = block * capacity, (block + 1) * capacity
        while row < end:
            owner = row // rows_per
            stop = min(end, (owner + 1) * rows_per)
            groups.append(
                (block, row // granule, (stop - row) // granule, owner,
                 (row - owner * rows_per) // granule)
            )
            row = stop
    return granule, groups


def kernel(
    n_exp, n_seq, chunks, tile, granule, groups,
    q_ref, lat_ref, kw_ref, og_ref, w_ref, hid_ref, up_ref, gate_ref, cnt_ref,
    vg_ref, hg_ref, wg_ref,
    q_v, lat_v, kw_v, g_v, w_v, hid_v, ups, own_sc, sc, sc_t, scale_v, acc, part, recv,
    load_sem, og_send, og_recv, up_send, up_recv, sc_send, sc_recv, part_send, part_recv,
):
    exp, seq = lax.axis_index("exp"), lax.axis_index("seq")
    step = n_exp // BLOCKS
    rows = hid_ref.shape[0]
    cap = rows // BLOCKS
    rows_per = rows // n_seq
    tokens, width = og_ref.shape[0], q_ref.shape[1]
    seq_len = q_ref.shape[0]

    def expert_at(distance):
        return lax.rem(exp + (distance % n_exp), n_exp)

    def seq_at(distance):
        return lax.rem(seq + (distance % n_seq), n_seq)

    offsets = sorted({(b * step * sign) % n_exp for b in range(BLOCKS) for sign in (1, -1)})
    partners = [(e, s) for e in offsets for s in range(n_seq) if (e, s) != (0, 0)]
    barrier = pltpu.get_barrier_semaphore()
    for e, s in partners:
        pl.semaphore_signal(
            barrier, inc=1, device_id={"exp": expert_at(e), "seq": seq_at(s)}, device_id_type=MESH
        )

    own_columns = pl.ds(pl.multiple_of(seq * width, width), width)
    own_tokens = pl.ds(pl.multiple_of(seq * tokens, tokens), tokens)
    loads = [
        pltpu.make_async_copy(hid_ref, hid_v, load_sem.at[0]),
        pltpu.make_async_copy(lat_ref, lat_v, load_sem.at[1]),
        pltpu.make_async_copy(kw_ref, kw_v, load_sem.at[2]),
        pltpu.make_async_copy(q_ref, q_v, load_sem.at[3]),
        pltpu.make_async_copy(og_ref.at[:, own_columns], g_v.at[own_tokens, :], load_sem.at[4]),
        pltpu.make_async_copy(up_ref.at[pl.ds(0, cap), :], ups.at[pl.ds(0, cap), :], load_sem.at[5]),
        pltpu.make_async_copy(w_ref, w_v, load_sem.at[6]),
    ]
    for load in loads:
        load.start()
    pl.semaphore_wait(barrier, len(partners))

    up_copies = []
    for c, (start, size) in enumerate(chunks):
        pair = []
        for b in (1, 2):
            place = (pl.ds(b * cap, cap), pl.ds(start, size))
            copy = pltpu.make_async_remote_copy(
                src_ref=up_ref.at[place], dst_ref=ups.at[place],
                send_sem=up_send.at[c, b - 1], recv_sem=up_recv.at[c, b - 1],
                device_id={"exp": expert_at(-b * step)}, device_id_type=MESH,
            )
            copy.start()
            pair.append(copy)
        up_copies.append(pair)
    og_copies = []
    for k in range(1, n_seq):
        other = seq_at(k)
        copy = pltpu.make_async_remote_copy(
            src_ref=og_ref.at[:, pl.ds(pl.multiple_of(other * width, width), width)],
            dst_ref=g_v.at[own_tokens, :],
            send_sem=og_send.at[k - 1], recv_sem=og_recv.at[k - 1],
            device_id={"seq": other}, device_id_type=MESH,
        )
        copy.start()
        og_copies.append(copy)

    loads[0].wait()
    line = lax.broadcasted_iota(jnp.int32, (rows, rows), 0)
    column = lax.broadcasted_iota(jnp.int32, (rows, rows), 1)
    gates = jnp.where(line == column, gate_ref[...], 0.0).sum(axis=1, keepdims=True)
    row = lax.broadcasted_iota(jnp.int32, (rows, 1), 0)
    limit = jnp.zeros((rows, 1), jnp.int32) + cnt_ref[0, 0]
    for b in range(1, BLOCKS):
        limit = jnp.where(row >= b * cap, b * cap + cnt_ref[0, b], limit)
    scale = jnp.where(row < limit, gates, 0.0)
    scale_v[...] = jnp.broadcast_to(scale, scale_v.shape)
    own_sc[...] = (scale * hid_v[...].astype(jnp.float32)).astype(jnp.bfloat16)
    sc_copies = []
    for b in (1, 2):
        place = pl.ds(b * cap, cap)
        copy = pltpu.make_async_remote_copy(
            src_ref=own_sc.at[place, :], dst_ref=sc.at[place, :],
            send_sem=sc_send.at[b - 1], recv_sem=sc_recv.at[b - 1],
            device_id={"exp": expert_at(-b * step)}, device_id_type=MESH,
        )
        copy.start()
        sc_copies.append(copy)
    sc[pl.ds(0, cap), :] = own_sc[pl.ds(0, cap), :]

    for load in loads[1:5]:
        load.wait()
    for copy in og_copies:
        copy.wait_recv()
    t_rows = min(256, seq_len)
    factor = 1.0 / math.sqrt(HEAD_DIM)

    @pl.loop(0, width // 256)
    def _(pair):
        columns = pl.ds(pl.multiple_of(pair * 256, 256), 256)
        keys = dot_of(lat_v[...], kw_v[:, columns]).astype(jnp.bfloat16)
        for half in range(2):
            head = pl.ds(pl.multiple_of(pair * 256 + half * HEAD_DIM, HEAD_DIM), HEAD_DIM)
            k_head = keys[:, half * HEAD_DIM : (half + 1) * HEAD_DIM]
            for first in range(0, seq_len, t_rows):
                last = first + t_rows
                q_head = q_v[pl.ds(first, t_rows), head]
                scores = lax.dot_general(
                    k_head[:last], q_head, LAST, preferred_element_type=jnp.float32
                ) * factor
                u = lax.broadcasted_iota(jnp.int32, scores.shape, 0)
                t = lax.broadcasted_iota(jnp.int32, scores.shape, 1) + first
                scores = jnp.where(u <= t, scores, -jnp.inf)
                weights = jnp.exp(scores - scores.max(axis=0, keepdims=True))
                probs = weights * (1.0 / weights.sum(axis=0, keepdims=True))
                term = dot_of(probs.astype(jnp.bfloat16), g_v[pl.ds(first, t_rows), head])
                total = term if first == 0 else term + jnp.concatenate(
                    [total, jnp.zeros((t_rows, HEAD_DIM), jnp.float32)], 0
                )
            vg_ref[:, head] = total.astype(jnp.bfloat16)

    loads[5].wait()
    loads[6].wait()
    for c, (start, size) in enumerate(chunks):
        for copy in up_copies[c]:
            copy.wait_recv()
        columns = pl.ds(start, size)
        product = lax.dot_general(
            ups[:, columns], w_v[:, columns], LAST, preferred_element_type=jnp.float32
        )
        acc[...] = product if c == 0 else acc[...] + product
    part[...] = acc[...].reshape(part.shape).astype(jnp.bfloat16)

    def group_copy(n):
        block, first, count, owner, place = groups[n]
        return pltpu.make_async_remote_copy(
            src_ref=part.at[pl.ds(first, count)],
            dst_ref=recv.at[seq, pl.ds(place, count)],
            send_sem=part_send.at[n], recv_sem=part_recv.at[seq, n],
            device_id={"exp": expert_at(block * step), "seq": owner}, device_id_type=MESH,
        )

    def arrival(n, source):
        block, first, count, owner, place = groups[n]
        return pltpu.make_async_remote_copy(
            src_ref=part.at[pl.ds(first, count)],
            dst_ref=recv.at[source, pl.ds(place, count)],
            send_sem=part_send.at[n], recv_sem=part_recv.at[source, n],
            device_id={"exp": expert_at(block * step), "seq": owner}, device_id_type=MESH,
        )

    for n in reversed(range(len(groups))):
        block, first, count, owner, place = groups[n]
        if block:
            group_copy(n).start()
        else:
            @pl.when(seq != owner)
            def _():
                group_copy(n).start()

            @pl.when(seq == owner)
            def _():
                recv[seq, pl.ds(place, count)] = part[pl.ds(first, count)]

    for copy in sc_copies:
        copy.wait_recv()
    sc_t[...] = sc[...].astype(jnp.float32).T.astype(jnp.bfloat16)

    @pl.loop(0, w_ref.shape[1] // tile)
    def _(n):
        columns = pl.ds(pl.multiple_of(n * tile, tile), tile)
        wg_ref[:, columns] = dot_of(sc_t[...], ups[:, columns]).astype(jnp.bfloat16)

    for n, (block, first, count, owner, place) in enumerate(groups):
        for source in range(n_seq):
            wanted = (seq == owner) if block else (seq == owner) & (seq != source)

            @pl.when(wanted)
            def _():
                arrival(n, source).wait_recv()
    total = recv[0].astype(jnp.float32)
    for source in range(1, n_seq):
        total = total + recv[source].astype(jnp.float32)
    own_rows = pl.ds(pl.multiple_of(seq * rows_per, 8), rows_per)
    hg_ref[...] = total.reshape(hg_ref.shape) * scale_v[own_rows, :][:, :1]

    for n, (block, first, count, owner, place) in enumerate(groups):
        if block:
            group_copy(n).wait_send()
        else:
            @pl.when(seq != owner)
            def _():
                group_copy(n).wait_send()
    for copy in sc_copies + og_copies + [c for pair in up_copies for c in pair]:
        copy.wait_send()


def on_device(
    queries, latent_rows, key_weight, output_grad, down_weight, hidden_rows, upstream_rows,
    row_gates, row_counts,
):
    n_exp, n_seq = lax.axis_size("exp"), lax.axis_size("seq")
    seq_len, width = queries.shape[1], queries.shape[3]
    tokens, latent = output_grad.shape[1], latent_rows.shape[2]
    hidden, model = down_weight.shape[1:]
    rows = hidden_rows.shape[0]
    rows_per = rows // n_seq
    granule, groups = grad_groups(rows // BLOCKS, rows_per)
    size = 512 if model % 512 == 0 else model
    tile = 512 if model % 512 == 0 else 128
    chunks = [(start, size) for start in range(0, model, size)]
    bf16, f32 = jnp.bfloat16, jnp.float32
    anywhere = pl.BlockSpec(memory_space=pltpu.HBM)
    vmem = pl.BlockSpec(memory_space=pltpu.VMEM)
    smem = pl.BlockSpec(memory_space=pltpu.SMEM)
    dma = pltpu.SemaphoreType.DMA
    value_grad, hidden_grad, weight_grad = pl.pallas_call(
        functools.partial(kernel, n_exp, n_seq, chunks, tile, granule, groups),
        out_shape=(
            pltpu.VMEM((seq_len, width), bf16),
            pltpu.VMEM((rows_per, hidden), f32),
            pltpu.VMEM((hidden, model), bf16),
        ),
        in_specs=[anywhere] * 7 + [vmem, smem],
        out_specs=(vmem,) * 3,
        scratch_shapes=[
            pltpu.VMEM((seq_len, width), bf16),
            pltpu.VMEM((seq_len, latent), bf16),
            pltpu.VMEM((latent, width), bf16),
            pltpu.VMEM((seq_len, width), bf16),
            pltpu.VMEM((hidden, model), bf16),
            pltpu.VMEM((rows, hidden), bf16),
            pltpu.VMEM((rows, model), bf16),
            pltpu.VMEM((rows, hidden), bf16),
            pltpu.VMEM((rows, hidden), bf16),
            pltpu.VMEM((hidden, rows), bf16),
            pltpu.VMEM((rows, 128), f32),
            pltpu.VMEM((rows, hidden), f32),
            pltpu.VMEM((rows // granule, granule, hidden), bf16),
            pltpu.VMEM((n_seq, rows_per // granule, granule, hidden), bf16),
            dma((7,)),
            dma((n_seq - 1,)),
            dma((n_seq - 1,)),
            dma((len(chunks), 2)),
            dma((len(chunks), 2)),
            dma((2,)),
            dma((2,)),
            dma((len(groups),)),
            dma((n_seq, len(groups))),
        ],
        compiler_params=pltpu.CompilerParams(
            collective_id=0, has_side_effects=True, vmem_limit_bytes=59 * 1024 * 1024
        ),
    )(
        queries.reshape(seq_len, width), latent_rows[0], key_weight.reshape(latent, width),
        output_grad.reshape(tokens, output_grad.shape[3]), down_weight[0], hidden_rows,
        upstream_rows, row_gates.reshape(1, rows), row_counts,
    )
    return (
        value_grad.reshape(1, seq_len, 1, width),
        hidden_grad,
        weight_grad[None],
    )


def solution(mesh):
    placed = (
        P("exp", None, "dp", "seq"),
        P("exp", None, None),
        P(None, "dp", "seq"),
        P("exp", "seq", "dp", None),
        P("exp", "dp", "seq"),
        P("exp", "dp"),
        P("exp", "seq"),
        P("exp"),
        P("exp", None),
    )
    return jax.shard_map(
        on_device,
        mesh=mesh,
        in_specs=placed,
        out_specs=(P("exp", None, "dp", "seq"), P(("exp", "seq"), "dp"), P("exp", "dp", "seq")),
        check_vma=False,
    )
```

```python
import functools
import math

import jax
import jax.numpy as jnp
from jax import lax
from jax.experimental import pallas as pl
from jax.experimental.pallas import tpu as pltpu
from jax.sharding import PartitionSpec as P

HEAD_DIM = 128
BLOCKS = 3
MESH = pl.DeviceIdType.MESH
LAST = (((1,), (1,)), ((), ()))


def dot_of(a, b):
    return jnp.dot(a, b, preferred_element_type=jnp.float32)


def grad_groups(capacity, rows_per):
    granule = math.gcd(capacity, rows_per)
    groups = []
    for block in range(BLOCKS):
        row, end = block * capacity, (block + 1) * capacity
        while row < end:
            owner = row // rows_per
            stop = min(end, (owner + 1) * rows_per)
            groups.append(
                (block, row // granule, (stop - row) // granule, owner,
                 (row - owner * rows_per) // granule)
            )
            row = stop
    return granule, groups


def kernel(
    n_exp, n_seq, size, tile, granule, groups,
    q_ref, lat_ref, kw_ref, og_ref, w_ref, hid_ref, up_ref, gate_ref, cnt_ref,
    vg_ref, hg_ref, wg_ref,
    q_v, lat_v, kw_v, g_v, w_v, hid_v, ups, own_sc, sc, sc_t, scale_v, acc, part, recv, probs_v,
    load_sem, og_send, og_recv, up_send, up_recv, near_send, far_send, far_recv, sc_send, sc_recv, part_send, part_recv,
):
    exp, seq, dp = lax.axis_index("exp"), lax.axis_index("seq"), lax.axis_index("dp")
    step = n_exp // BLOCKS
    rows = hid_ref.shape[0]
    cap = rows // BLOCKS
    rows_per = rows // n_seq
    tokens, width = og_ref.shape[0], q_ref.shape[1]
    seq_len = q_ref.shape[0]

    def expert_at(distance):
        return lax.rem(exp + (distance % n_exp), n_exp)

    def seq_at(distance):
        return lax.rem(seq + (distance % n_seq), n_seq)

    offsets = sorted({(b * step * sign) % n_exp for b in range(BLOCKS) for sign in (1, -1)})
    partners = [(e, s) for e in offsets for s in range(n_seq) if (e, s) != (0, 0)]
    side = lax.rem(dp, 2)
    mate = dp + 1 - 2 * side
    n_chunks = w_ref.shape[1] // size
    barrier = pltpu.get_barrier_semaphore()
    pl.semaphore_signal(barrier, inc=1, device_id={"dp": mate}, device_id_type=MESH)
    for e, s in partners:
        pl.semaphore_signal(
            barrier, inc=1, device_id={"exp": expert_at(e), "seq": seq_at(s)}, device_id_type=MESH
        )

    own_columns = pl.ds(pl.multiple_of(seq * width, width), width)
    own_tokens = pl.ds(pl.multiple_of(seq * tokens, tokens), tokens)
    loads = [
        pltpu.make_async_copy(hid_ref, hid_v, load_sem.at[0]),
        pltpu.make_async_copy(lat_ref, lat_v, load_sem.at[1]),
        pltpu.make_async_copy(kw_ref, kw_v, load_sem.at[2]),
        pltpu.make_async_copy(q_ref, q_v, load_sem.at[3]),
        pltpu.make_async_copy(og_ref.at[:, own_columns], g_v.at[own_tokens, :], load_sem.at[4]),
        pltpu.make_async_copy(up_ref.at[pl.ds(0, cap), :], ups.at[pl.ds(0, cap), :], load_sem.at[5]),
        pltpu.make_async_copy(w_ref, w_v, load_sem.at[6]),
    ]
    for load in loads:
        load.start()
    pl.semaphore_wait(barrier, len(partners) + 1)

    half = cap // 2
    near_to = (step == 1) & (lax.rem(exp, 2) == 1)
    near_from = (step == 1) & (lax.rem(exp, 2) == 0)

    def share(c, b, which):
        return (
            pl.ds(pl.multiple_of(b * cap + which * half, half), half),
            pl.ds(pl.multiple_of(c * size, 128), size),
        )

    def direct(c, b):
        place = share(c, b, side)
        return pltpu.make_async_remote_copy(
            src_ref=up_ref.at[place], dst_ref=ups.at[place],
            send_sem=up_send.at[c, b - 1], recv_sem=up_recv.at[c, b - 1],
            device_id={"exp": expert_at(-b * step)}, device_id_type=MESH,
        )

    def near(c):
        place = share(c, 1, 1 - side)
        return pltpu.make_async_remote_copy(
            src_ref=up_ref.at[place], dst_ref=ups.at[place],
            send_sem=near_send.at[c], recv_sem=far_recv.at[c, 0],
            device_id={"exp": expert_at(-step)}, device_id_type=MESH,
        )

    def forward(c, b, which):
        place = share(c, b, which)
        return pltpu.make_async_remote_copy(
            src_ref=ups.at[place], dst_ref=ups.at[place],
            send_sem=far_send.at[c, b - 1], recv_sem=far_recv.at[c, b - 1],
            device_id={"dp": mate}, device_id_type=MESH,
        )

    for c in range(n_chunks):
        direct(c, 1).start()
        direct(c, 2).start()
    if step == 1:
        @pl.when(near_to)
        def _():
            for c in range(n_chunks):
                near(c).start()
    og_copies = []
    for k in range(1, n_seq):
        other = seq_at(k)
        copy = pltpu.make_async_remote_copy(
            src_ref=og_ref.at[:, pl.ds(pl.multiple_of(other * width, width), width)],
            dst_ref=g_v.at[own_tokens, :],
            send_sem=og_send.at[k - 1], recv_sem=og_recv.at[k - 1],
            device_id={"seq": other}, device_id_type=MESH,
        )
        copy.start()
        og_copies.append(copy)

    loads[0].wait()
    line = lax.broadcasted_iota(jnp.int32, (rows, rows), 0)
    column = lax.broadcasted_iota(jnp.int32, (rows, rows), 1)
    gates = jnp.where(line == column, gate_ref[...], 0.0).sum(axis=1, keepdims=True)
    row = lax.broadcasted_iota(jnp.int32, (rows, 1), 0)
    limit = jnp.zeros((rows, 1), jnp.int32) + cnt_ref[0, 0]
    for b in range(1, BLOCKS):
        limit = jnp.where(row >= b * cap, b * cap + cnt_ref[0, b], limit)
    scale = jnp.where(row < limit, gates, 0.0)
    scale_v[...] = jnp.broadcast_to(scale, scale_v.shape)
    own_sc[...] = (scale * hid_v[...].astype(jnp.float32)).astype(jnp.bfloat16)
    sc_copies = []
    for b in (1, 2):
        place = pl.ds(b * cap, cap)
        copy = pltpu.make_async_remote_copy(
            src_ref=own_sc.at[place, :], dst_ref=sc.at[place, :],
            send_sem=sc_send.at[b - 1], recv_sem=sc_recv.at[b - 1],
            device_id={"exp": expert_at(-b * step)}, device_id_type=MESH,
        )
        copy.start()
        sc_copies.append(copy)
    sc[pl.ds(0, cap), :] = own_sc[pl.ds(0, cap), :]

    for load in loads[1:4]:
        load.wait()
    t_rows = min(256, seq_len)
    factor = 1.0 / math.sqrt(HEAD_DIM)
    pairs = width // 256
    per_pair = -(-n_chunks // pairs)

    @pl.loop(0, pairs)
    def _(pair):
        columns = pl.ds(pl.multiple_of(pair * 256, 256), 256)
        keys = dot_of(lat_v[...], kw_v[:, columns]).astype(jnp.bfloat16)
        for member in range(2):
            head = pl.ds(pl.multiple_of(pair * 256 + member * HEAD_DIM, HEAD_DIM), HEAD_DIM)
            k_head = keys[:, member * HEAD_DIM : (member + 1) * HEAD_DIM]
            for first in range(0, seq_len, t_rows):
                last = first + t_rows
                q_head = q_v[pl.ds(first, t_rows), head]
                scores = lax.dot_general(
                    k_head[:last], q_head, LAST, preferred_element_type=jnp.float32
                ) * factor
                u = lax.broadcasted_iota(jnp.int32, scores.shape, 0)
                t = lax.broadcasted_iota(jnp.int32, scores.shape, 1) + first
                scores = jnp.where(u <= t, scores, -jnp.inf)
                weights = jnp.exp(scores - scores.max(axis=0, keepdims=True))
                probs = weights * (1.0 / weights.sum(axis=0, keepdims=True))
                probs_v[2 * pair + member, pl.ds(0, last), pl.ds(first, t_rows)] = probs.astype(
                    jnp.bfloat16
                )
        for i in range(per_pair):
            c = pair * per_pair + i

            @pl.when(c < n_chunks)
            def _():
                for b in (2, 1):
                    direct(c, b).wait_recv()
                    if b == 1 and step == 1:
                        @pl.when(jnp.logical_not(near_from))
                        def _():
                            forward(c, b, side).start()
                    else:
                        forward(c, b, side).start()

    loads[5].wait()
    loads[6].wait()
    for c in range(n_chunks):
        for b in (1, 2):
            forward(c, b, 1 - side).wait_recv()
        columns = pl.ds(c * size, size)
        product = lax.dot_general(
            ups[:, columns], w_v[:, columns], LAST, preferred_element_type=jnp.float32
        )
        acc[...] = product if c == 0 else acc[...] + product
    part[...] = acc[...].reshape(part.shape).astype(jnp.bfloat16)

    def group_copy(n):
        block, first, count, owner, place = groups[n]
        return pltpu.make_async_remote_copy(
            src_ref=part.at[pl.ds(first, count)],
            dst_ref=recv.at[seq, pl.ds(place, count)],
            send_sem=part_send.at[n], recv_sem=part_recv.at[seq, n],
            device_id={"exp": expert_at(block * step), "seq": owner}, device_id_type=MESH,
        )

    def arrival(n, source):
        block, first, count, owner, place = groups[n]
        return pltpu.make_async_remote_copy(
            src_ref=part.at[pl.ds(first, count)],
            dst_ref=recv.at[source, pl.ds(place, count)],
            send_sem=part_send.at[n], recv_sem=part_recv.at[source, n],
            device_id={"exp": expert_at(block * step), "seq": owner}, device_id_type=MESH,
        )

    for n in reversed(range(len(groups))):
        block, first, count, owner, place = groups[n]
        if block:
            group_copy(n).start()
        else:
            @pl.when(seq != owner)
            def _():
                group_copy(n).start()

            @pl.when(seq == owner)
            def _():
                recv[seq, pl.ds(place, count)] = part[pl.ds(first, count)]

    loads[4].wait()
    for copy in og_copies:
        copy.wait_recv()

    @pl.loop(0, width // HEAD_DIM)
    def _(h):
        head = pl.ds(pl.multiple_of(h * HEAD_DIM, HEAD_DIM), HEAD_DIM)
        total = None
        for first in range(0, seq_len, t_rows):
            term = dot_of(
                probs_v[h, pl.ds(0, first + t_rows), pl.ds(first, t_rows)],
                g_v[pl.ds(first, t_rows), head],
            )
            total = term if first == 0 else term + jnp.concatenate(
                [total, jnp.zeros((t_rows, HEAD_DIM), jnp.float32)], 0
            )
        vg_ref[:, head] = total.astype(jnp.bfloat16)

    for copy in sc_copies:
        copy.wait_recv()
    sc_t[...] = sc[...].astype(jnp.float32).T.astype(jnp.bfloat16)

    @pl.loop(0, w_ref.shape[1] // tile)
    def _(n):
        columns = pl.ds(pl.multiple_of(n * tile, tile), tile)
        wg_ref[:, columns] = dot_of(sc_t[...], ups[:, columns]).astype(jnp.bfloat16)

    for n, (block, first, count, owner, place) in enumerate(groups):
        for source in range(n_seq):
            wanted = (seq == owner) if block else (seq == owner) & (seq != source)

            @pl.when(wanted)
            def _():
                arrival(n, source).wait_recv()
    total = recv[0].astype(jnp.float32)
    for source in range(1, n_seq):
        total = total + recv[source].astype(jnp.float32)
    own_rows = pl.ds(pl.multiple_of(seq * rows_per, 8), rows_per)
    hg_ref[...] = total.reshape(hg_ref.shape) * scale_v[own_rows, :][:, :1]

    for n, (block, first, count, owner, place) in enumerate(groups):
        if block:
            group_copy(n).wait_send()
        else:
            @pl.when(seq != owner)
            def _():
                group_copy(n).wait_send()
    for copy in sc_copies + og_copies:
        copy.wait_send()
    for c in range(n_chunks):
        direct(c, 1).wait_send()
        direct(c, 2).wait_send()
        forward(c, 2, side).wait_send()
        if step == 1:
            @pl.when(near_to)
            def _():
                near(c).wait_send()
                forward(c, 1, side).wait_send()
        else:
            forward(c, 1, side).wait_send()


def on_device(
    queries, latent_rows, key_weight, output_grad, down_weight, hidden_rows, upstream_rows,
    row_gates, row_counts,
):
    n_exp, n_seq = lax.axis_size("exp"), lax.axis_size("seq")
    seq_len, width = queries.shape[1], queries.shape[3]
    tokens, latent = output_grad.shape[1], latent_rows.shape[2]
    hidden, model = down_weight.shape[1:]
    rows = hidden_rows.shape[0]
    rows_per = rows // n_seq
    granule, groups = grad_groups(rows // BLOCKS, rows_per)
    size = 512 if model % 512 == 0 else model
    tile = 512 if model % 512 == 0 else 128
    n_chunks = model // size
    bf16, f32 = jnp.bfloat16, jnp.float32
    anywhere = pl.BlockSpec(memory_space=pltpu.HBM)
    vmem = pl.BlockSpec(memory_space=pltpu.VMEM)
    smem = pl.BlockSpec(memory_space=pltpu.SMEM)
    dma = pltpu.SemaphoreType.DMA
    value_grad, hidden_grad, weight_grad = pl.pallas_call(
        functools.partial(kernel, n_exp, n_seq, size, tile, granule, groups),
        out_shape=(
            pltpu.VMEM((seq_len, width), bf16),
            pltpu.VMEM((rows_per, hidden), f32),
            pltpu.VMEM((hidden, model), bf16),
        ),
        in_specs=[anywhere] * 7 + [vmem, smem],
        out_specs=(vmem,) * 3,
        scratch_shapes=[
            pltpu.VMEM((seq_len, width), bf16),
            pltpu.VMEM((seq_len, latent), bf16),
            pltpu.VMEM((latent, width), bf16),
            pltpu.VMEM((seq_len, width), bf16),
            pltpu.VMEM((hidden, model), bf16),
            pltpu.VMEM((rows, hidden), bf16),
            pltpu.VMEM((rows, model), bf16),
            pltpu.VMEM((rows, hidden), bf16),
            pltpu.VMEM((rows, hidden), bf16),
            pltpu.VMEM((hidden, rows), bf16),
            pltpu.VMEM((rows, 128), f32),
            pltpu.VMEM((rows, hidden), f32),
            pltpu.VMEM((rows // granule, granule, hidden), bf16),
            pltpu.VMEM((n_seq, rows_per // granule, granule, hidden), bf16),
            pltpu.VMEM((width // HEAD_DIM, seq_len, seq_len), bf16),
            dma((7,)),
            dma((n_seq - 1,)),
            dma((n_seq - 1,)),
            dma((n_chunks, 2)),
            dma((n_chunks, 2)),
            dma((n_chunks,)),
            dma((n_chunks, 2)),
            dma((n_chunks, 2)),
            dma((2,)),
            dma((2,)),
            dma((len(groups),)),
            dma((n_seq, len(groups))),
        ],
        compiler_params=pltpu.CompilerParams(
            collective_id=0, has_side_effects=True, vmem_limit_bytes=59 * 1024 * 1024
        ),
    )(
        queries.reshape(seq_len, width), latent_rows[0], key_weight.reshape(latent, width),
        output_grad.reshape(tokens, output_grad.shape[3]), down_weight[0], hidden_rows,
        upstream_rows, row_gates.reshape(1, rows), row_counts,
    )
    return (
        value_grad.reshape(1, seq_len, 1, width),
        hidden_grad,
        weight_grad[None],
    )


def solution(mesh):
    placed = (
        P("exp", None, "dp", "seq"),
        P("exp", None, None),
        P(None, "dp", "seq"),
        P("exp", "seq", "dp", None),
        P("exp", "dp", "seq"),
        P("exp", "dp"),
        P("exp", "seq"),
        P("exp"),
        P("exp", None),
    )
    return jax.shard_map(
        on_device,
        mesh=mesh,
        in_specs=placed,
        out_specs=(P("exp", None, "dp", "seq"), P(("exp", "seq"), "dp"), P("exp", "dp", "seq")),
        check_vma=False,
    )
```

```python
import functools
import math

import jax
import jax.numpy as jnp
from jax import lax
from jax.experimental import pallas as pl
from jax.experimental.pallas import tpu as pltpu
from jax.sharding import PartitionSpec as P

HEAD_DIM = 128
BLOCKS = 3
MESH = pl.DeviceIdType.MESH
LAST = (((1,), (1,)), ((), ()))


def dot_of(a, b):
    return jnp.dot(a, b, preferred_element_type=jnp.float32)


def grad_groups(capacity, rows_per):
    granule = math.gcd(capacity, rows_per)
    groups = []
    for block in range(BLOCKS):
        row, end = block * capacity, (block + 1) * capacity
        while row < end:
            owner = row // rows_per
            stop = min(end, (owner + 1) * rows_per)
            groups.append(
                (block, row // granule, (stop - row) // granule, owner,
                 (row - owner * rows_per) // granule)
            )
            row = stop
    return granule, groups


def kernel(
    n_exp, n_seq, size, tile, granule, groups,
    q_ref, lat_ref, kw_ref, og_ref, w_ref, hid_ref, up_ref, gate_ref, cnt_ref,
    vg_ref, hg_ref, wg_ref,
    q_v, lat_v, kw_v, g_v, w_v, hid_v, ups, own_sc, sc, sc_t, scale_v, acc, part, recv, probs_v,
    load_sem, og_send, og_recv, up_send, up_recv, near_send, far_send, far_recv, sc_send, sc_recv, part_send, part_recv,
):
    exp, seq, dp = lax.axis_index("exp"), lax.axis_index("seq"), lax.axis_index("dp")
    step = n_exp // BLOCKS
    rows = hid_ref.shape[0]
    cap = rows // BLOCKS
    rows_per = rows // n_seq
    tokens, width = og_ref.shape[0], q_ref.shape[1]
    seq_len = q_ref.shape[0]

    def expert_at(distance):
        return lax.rem(exp + (distance % n_exp), n_exp)

    def seq_at(distance):
        return lax.rem(seq + (distance % n_seq), n_seq)

    offsets = sorted({(b * step * sign) % n_exp for b in range(BLOCKS) for sign in (1, -1)})
    partners = [(e, s) for e in offsets for s in range(n_seq) if (e, s) != (0, 0)]
    side = lax.rem(dp, 2)
    mate = dp + 1 - 2 * side
    n_chunks = w_ref.shape[1] // size
    barrier = pltpu.get_barrier_semaphore()
    pl.semaphore_signal(barrier, inc=1, device_id={"dp": mate}, device_id_type=MESH)
    for e, s in partners:
        pl.semaphore_signal(
            barrier, inc=1, device_id={"exp": expert_at(e), "seq": seq_at(s)}, device_id_type=MESH
        )

    own_columns = pl.ds(pl.multiple_of(seq * width, width), width)
    own_tokens = pl.ds(pl.multiple_of(seq * tokens, tokens), tokens)
    loads = [
        pltpu.make_async_copy(hid_ref, hid_v, load_sem.at[0]),
        pltpu.make_async_copy(lat_ref, lat_v, load_sem.at[1]),
        pltpu.make_async_copy(kw_ref, kw_v, load_sem.at[2]),
        pltpu.make_async_copy(q_ref, q_v, load_sem.at[3]),
        pltpu.make_async_copy(og_ref.at[:, own_columns], g_v.at[own_tokens, :], load_sem.at[4]),
        pltpu.make_async_copy(up_ref.at[pl.ds(0, cap), :], ups.at[pl.ds(0, cap), :], load_sem.at[5]),
        pltpu.make_async_copy(w_ref, w_v, load_sem.at[6]),
    ]
    for load in loads:
        load.start()
    pl.semaphore_wait(barrier, len(partners) + 1)

    half = cap // 2
    near_to = (step == 1) & (lax.rem(exp, 2) == 1)
    near_from = (step == 1) & (lax.rem(exp, 2) == 0)

    def share(c, b, which):
        return (
            pl.ds(pl.multiple_of(b * cap + which * half, half), half),
            pl.ds(pl.multiple_of(c * size, 128), size),
        )

    def direct(c, b):
        place = share(c, b, side)
        return pltpu.make_async_remote_copy(
            src_ref=up_ref.at[place], dst_ref=ups.at[place],
            send_sem=up_send.at[c, b - 1], recv_sem=up_recv.at[c, b - 1],
            device_id={"exp": expert_at(-b * step)}, device_id_type=MESH,
        )

    def near(c):
        place = share(c, 1, 1 - side)
        return pltpu.make_async_remote_copy(
            src_ref=up_ref.at[place], dst_ref=ups.at[place],
            send_sem=near_send.at[c], recv_sem=far_recv.at[c, 0],
            device_id={"exp": expert_at(-step)}, device_id_type=MESH,
        )

    def forward(c, b, which):
        place = share(c, b, which)
        return pltpu.make_async_remote_copy(
            src_ref=ups.at[place], dst_ref=ups.at[place],
            send_sem=far_send.at[c, b - 1], recv_sem=far_recv.at[c, b - 1],
            device_id={"dp": mate}, device_id_type=MESH,
        )

    for c in range(n_chunks):
        direct(c, 1).start()
        direct(c, 2).start()
    if step == 1:
        @pl.when(near_to)
        def _():
            for c in range(n_chunks):
                near(c).start()
    og_copies = []
    for k in range(1, n_seq):
        other = seq_at(k)
        copy = pltpu.make_async_remote_copy(
            src_ref=og_ref.at[:, pl.ds(pl.multiple_of(other * width, width), width)],
            dst_ref=g_v.at[own_tokens, :],
            send_sem=og_send.at[k - 1], recv_sem=og_recv.at[k - 1],
            device_id={"seq": other}, device_id_type=MESH,
        )
        copy.start()
        og_copies.append(copy)

    loads[0].wait()
    line = lax.broadcasted_iota(jnp.int32, (rows, rows), 0)
    column = lax.broadcasted_iota(jnp.int32, (rows, rows), 1)
    gates = jnp.where(line == column, gate_ref[...], 0.0).sum(axis=1, keepdims=True)
    row = lax.broadcasted_iota(jnp.int32, (rows, 1), 0)
    limit = jnp.zeros((rows, 1), jnp.int32) + cnt_ref[0, 0]
    for b in range(1, BLOCKS):
        limit = jnp.where(row >= b * cap, b * cap + cnt_ref[0, b], limit)
    scale = jnp.where(row < limit, gates, 0.0)
    scale_v[...] = jnp.broadcast_to(scale, scale_v.shape)
    own_sc[...] = (scale * hid_v[...].astype(jnp.float32)).astype(jnp.bfloat16)
    sc_copies = []
    for b in (1, 2):
        place = pl.ds(b * cap, cap)
        copy = pltpu.make_async_remote_copy(
            src_ref=own_sc.at[place, :], dst_ref=sc.at[place, :],
            send_sem=sc_send.at[b - 1], recv_sem=sc_recv.at[b - 1],
            device_id={"exp": expert_at(-b * step)}, device_id_type=MESH,
        )
        copy.start()
        sc_copies.append(copy)
    sc[pl.ds(0, cap), :] = own_sc[pl.ds(0, cap), :]

    for load in loads[1:4]:
        load.wait()
    t_rows = min(256, seq_len)
    factor = 1.0 / math.sqrt(HEAD_DIM)
    pairs = width // 256
    per_pair = -(-n_chunks // pairs)

    @pl.loop(0, pairs)
    def _(pair):
        columns = pl.ds(pl.multiple_of(pair * 256, 256), 256)
        keys = dot_of(lat_v[...], kw_v[:, columns]).astype(jnp.bfloat16)
        for member in range(2):
            head = pl.ds(pl.multiple_of(pair * 256 + member * HEAD_DIM, HEAD_DIM), HEAD_DIM)
            k_head = keys[:, member * HEAD_DIM : (member + 1) * HEAD_DIM]
            for first in range(0, seq_len, t_rows):
                last = first + t_rows
                q_head = q_v[pl.ds(first, t_rows), head]
                scores = lax.dot_general(
                    k_head[:last], q_head, LAST, preferred_element_type=jnp.float32
                ) * factor
                u = lax.broadcasted_iota(jnp.int32, scores.shape, 0)
                t = lax.broadcasted_iota(jnp.int32, scores.shape, 1) + first
                scores = jnp.where(u <= t, scores, -jnp.inf)
                weights = jnp.exp(scores - scores.max(axis=0, keepdims=True))
                probs = weights * (1.0 / weights.sum(axis=0, keepdims=True))
                probs_v[2 * pair + member, pl.ds(0, last), pl.ds(first, t_rows)] = probs.astype(
                    jnp.bfloat16
                )
        for i in range(per_pair):
            c = pair * per_pair + i

            @pl.when(c < n_chunks)
            def _():
                for b in (2, 1):
                    direct(c, b).wait_recv()
                    if b == 1 and step == 1:
                        @pl.when(jnp.logical_not(near_from))
                        def _():
                            forward(c, b, side).start()
                    else:
                        forward(c, b, side).start()

    loads[4].wait()
    for copy in og_copies:
        copy.wait_recv()

    @pl.loop(0, width // HEAD_DIM)
    def _(h):
        head = pl.ds(pl.multiple_of(h * HEAD_DIM, HEAD_DIM), HEAD_DIM)
        total = None
        for first in range(0, seq_len, t_rows):
            term = dot_of(
                probs_v[h, pl.ds(0, first + t_rows), pl.ds(first, t_rows)],
                g_v[pl.ds(first, t_rows), head],
            )
            total = term if first == 0 else term + jnp.concatenate(
                [total, jnp.zeros((t_rows, HEAD_DIM), jnp.float32)], 0
            )
        vg_ref[:, head] = total.astype(jnp.bfloat16)

    lag = 3

    def weigh(c):
        if c == 0:
            for copy in sc_copies:
                copy.wait_recv()
            sc_t[...] = sc[...].astype(jnp.float32).T.astype(jnp.bfloat16)
        for start in range(c * size, (c + 1) * size, tile):
            columns = pl.ds(start, tile)
            wg_ref[:, columns] = dot_of(sc_t[...], ups[:, columns]).astype(jnp.bfloat16)

    loads[5].wait()
    loads[6].wait()
    for c in range(n_chunks):
        for b in (1, 2):
            forward(c, b, 1 - side).wait_recv()
        columns = pl.ds(c * size, size)
        product = lax.dot_general(
            ups[:, columns], w_v[:, columns], LAST, preferred_element_type=jnp.float32
        )
        acc[...] = product if c == 0 else acc[...] + product
        if c >= lag:
            weigh(c - lag)
    part[...] = acc[...].reshape(part.shape).astype(jnp.bfloat16)

    def group_copy(n):
        block, first, count, owner, place = groups[n]
        return pltpu.make_async_remote_copy(
            src_ref=part.at[pl.ds(first, count)],
            dst_ref=recv.at[seq, pl.ds(place, count)],
            send_sem=part_send.at[n], recv_sem=part_recv.at[seq, n],
            device_id={"exp": expert_at(block * step), "seq": owner}, device_id_type=MESH,
        )

    def arrival(n, source):
        block, first, count, owner, place = groups[n]
        return pltpu.make_async_remote_copy(
            src_ref=part.at[pl.ds(first, count)],
            dst_ref=recv.at[source, pl.ds(place, count)],
            send_sem=part_send.at[n], recv_sem=part_recv.at[source, n],
            device_id={"exp": expert_at(block * step), "seq": owner}, device_id_type=MESH,
        )

    for n in reversed(range(len(groups))):
        block, first, count, owner, place = groups[n]
        if block:
            group_copy(n).start()
        else:
            @pl.when(seq != owner)
            def _():
                group_copy(n).start()

            @pl.when(seq == owner)
            def _():
                recv[seq, pl.ds(place, count)] = part[pl.ds(first, count)]

    for c in range(max(0, n_chunks - lag), n_chunks):
        weigh(c)

    for n, (block, first, count, owner, place) in enumerate(groups):
        for source in range(n_seq):
            wanted = (seq == owner) if block else (seq == owner) & (seq != source)

            @pl.when(wanted)
            def _():
                arrival(n, source).wait_recv()
    total = recv[0].astype(jnp.float32)
    for source in range(1, n_seq):
        total = total + recv[source].astype(jnp.float32)
    own_rows = pl.ds(pl.multiple_of(seq * rows_per, 8), rows_per)
    hg_ref[...] = total.reshape(hg_ref.shape) * scale_v[own_rows, :][:, :1]

    for n, (block, first, count, owner, place) in enumerate(groups):
        if block:
            group_copy(n).wait_send()
        else:
            @pl.when(seq != owner)
            def _():
                group_copy(n).wait_send()
    for copy in sc_copies + og_copies:
        copy.wait_send()
    for c in range(n_chunks):
        direct(c, 1).wait_send()
        direct(c, 2).wait_send()
        forward(c, 2, side).wait_send()
        if step == 1:
            @pl.when(near_to)
            def _():
                near(c).wait_send()
                forward(c, 1, side).wait_send()
        else:
            forward(c, 1, side).wait_send()


def on_device(
    queries, latent_rows, key_weight, output_grad, down_weight, hidden_rows, upstream_rows,
    row_gates, row_counts,
):
    n_exp, n_seq = lax.axis_size("exp"), lax.axis_size("seq")
    seq_len, width = queries.shape[1], queries.shape[3]
    tokens, latent = output_grad.shape[1], latent_rows.shape[2]
    hidden, model = down_weight.shape[1:]
    rows = hidden_rows.shape[0]
    rows_per = rows // n_seq
    granule, groups = grad_groups(rows // BLOCKS, rows_per)
    size = 512 if model % 512 == 0 else model
    tile = 512 if model % 512 == 0 else 128
    n_chunks = model // size
    bf16, f32 = jnp.bfloat16, jnp.float32
    anywhere = pl.BlockSpec(memory_space=pltpu.HBM)
    vmem = pl.BlockSpec(memory_space=pltpu.VMEM)
    smem = pl.BlockSpec(memory_space=pltpu.SMEM)
    dma = pltpu.SemaphoreType.DMA
    value_grad, hidden_grad, weight_grad = pl.pallas_call(
        functools.partial(kernel, n_exp, n_seq, size, tile, granule, groups),
        out_shape=(
            pltpu.VMEM((seq_len, width), bf16),
            pltpu.VMEM((rows_per, hidden), f32),
            pltpu.VMEM((hidden, model), bf16),
        ),
        in_specs=[anywhere] * 7 + [vmem, smem],
        out_specs=(vmem,) * 3,
        scratch_shapes=[
            pltpu.VMEM((seq_len, width), bf16),
            pltpu.VMEM((seq_len, latent), bf16),
            pltpu.VMEM((latent, width), bf16),
            pltpu.VMEM((seq_len, width), bf16),
            pltpu.VMEM((hidden, model), bf16),
            pltpu.VMEM((rows, hidden), bf16),
            pltpu.VMEM((rows, model), bf16),
            pltpu.VMEM((rows, hidden), bf16),
            pltpu.VMEM((rows, hidden), bf16),
            pltpu.VMEM((hidden, rows), bf16),
            pltpu.VMEM((rows, 128), f32),
            pltpu.VMEM((rows, hidden), f32),
            pltpu.VMEM((rows // granule, granule, hidden), bf16),
            pltpu.VMEM((n_seq, rows_per // granule, granule, hidden), bf16),
            pltpu.VMEM((width // HEAD_DIM, seq_len, seq_len), bf16),
            dma((7,)),
            dma((n_seq - 1,)),
            dma((n_seq - 1,)),
            dma((n_chunks, 2)),
            dma((n_chunks, 2)),
            dma((n_chunks,)),
            dma((n_chunks, 2)),
            dma((n_chunks, 2)),
            dma((2,)),
            dma((2,)),
            dma((len(groups),)),
            dma((n_seq, len(groups))),
        ],
        compiler_params=pltpu.CompilerParams(
            collective_id=0, has_side_effects=True, vmem_limit_bytes=59 * 1024 * 1024
        ),
    )(
        queries.reshape(seq_len, width), latent_rows[0], key_weight.reshape(latent, width),
        output_grad.reshape(tokens, output_grad.shape[3]), down_weight[0], hidden_rows,
        upstream_rows, row_gates.reshape(1, rows), row_counts,
    )
    return (
        value_grad.reshape(1, seq_len, 1, width),
        hidden_grad,
        weight_grad[None],
    )


def solution(mesh):
    placed = (
        P("exp", None, "dp", "seq"),
        P("exp", None, None),
        P(None, "dp", "seq"),
        P("exp", "seq", "dp", None),
        P("exp", "dp", "seq"),
        P("exp", "dp"),
        P("exp", "seq"),
        P("exp"),
        P("exp", None),
    )
    return jax.shard_map(
        on_device,
        mesh=mesh,
        in_specs=placed,
        out_specs=(P("exp", None, "dp", "seq"), P(("exp", "seq"), "dp"), P("exp", "dp", "seq")),
        check_vma=False,
    )
```
